32 devices in a mesh: grp: 4 (over z), cell: 8 (over y, x, core).
Axes of the slice: x: 2, y: 2, z: 4, core: 2. Of those that a mesh axis runs over, the one named last changes fastest.
Arguments:
- load: float32 [32, 2048, 256], P(('grp', 'cell')), may hold values from -6 to 6
- schur: bfloat16 [32, 2048, 2048], P(('grp', 'cell')), as said below
- local_inverse: bfloat16 [32, 2048, 2048], P(('grp', 'cell')), as said below
- face_map: int32 [32, 4, 512], P(('grp', 'cell')), may hold values from 0 to 511, as said below
- primal_basis: bfloat16 [32, 32, 2048], P(('grp', 'cell')), may hold values from -0.25 to 0.25
- primal_index: int32 [32, 32], P(('grp', 'cell')), may hold values from 0 to 255
- group_inverse: float32 [4, 256, 256], P('grp', 'cell'), as said below
- group_to_coarsest: float32 [4, 256, 128], P('grp', 'cell'), may hold values from -0.375 to 0.375
- coarsest_inverse: float32 [128, 128], replicated, as said below
Outputs:
- solution: float32 [32, 2048, 256], P(('grp', 'cell'))
- residual: float32 [32, 2048, 256], P(('grp', 'cell'))
The draws below stay inside these ranges and needn't reach their ends.
Inputs may be any that keep to these rules, and one draw needn't show every extreme that they name: face_map[i, f] is a permutation of 0 .. 511, and the maps of two neighbouring cells across their shared face are inverse to each other. `schur`: each cell's matrix is symmetric positive definite. `local_inverse`: each cell's matrix is symmetric positive definite. `group_inverse`: each row's matrix is symmetric positive definite. `coarsest_inverse`: symmetric positive definite.
All inputs are finite; a program needn't handle non-finite values.
Results may differ from the reference program's by a relative error of at most 0.0066.
Values sent between devices are 32-bit elements; how exact they have to be, the bound alone decides.
No kernel may reach another device: no remote copies, remote signals or barrier semaphores. Data moves between devices by JAX's collectives and lax.ppermute only.
A program may use at most 128 MiB of HBM per device.

```python
import math
import jax
import jax.numpy as jnp
from jax import lax

IFACE = 2048
FACE = 512
RHS = 256
PRIM = 32
NQ = 128
ITERS = 2
LAT_ROWS = 4
LAT_COLS = 8
CELLS = 32
NCG = 256


def one_definite(key, order, center, spread):
    noise = jax.random.normal(jax.random.fold_in(key, 1), (order, order), jnp.float32)
    matrix = (noise + noise.T) * (spread / math.sqrt(2.0 * order)) + center * jnp.eye(order, dtype=jnp.float32)
    return matrix


def stack_definite(key, count, order, center, spread):
    keys = jax.random.split(key, count)
    return lax.map(lambda single: one_definite(single, order, center, spread), keys)


def draw_schur(key, part):
    return stack_definite(jax.random.fold_in(key, 11), CELLS, IFACE, 2.0, 0.6).astype(jnp.bfloat16)


def draw_local_inverse(key, part):
    return stack_definite(jax.random.fold_in(key, 12), CELLS, IFACE, 0.5, 0.15).astype(jnp.bfloat16)


def draw_group_inverse(key, part):
    return stack_definite(jax.random.fold_in(key, 13), LAT_ROWS, NCG, 1.0, 0.3)


def draw_coarsest_inverse(key, part):
    return stack_definite(jax.random.fold_in(key, 14), 1, NQ, 0.5, 0.15)[0]


def draw_face_map(key, part):
    keys = jax.random.split(jax.random.fold_in(key, 15), 4 * CELLS)
    perms = jax.vmap(lambda single: jax.random.permutation(single, FACE))(keys).astype(jnp.int32)
    across = perms[:CELLS].reshape(LAT_ROWS, LAT_COLS, FACE)
    upward = perms[CELLS:2 * CELLS].reshape(LAT_ROWS, LAT_COLS, FACE)
    spare_west = perms[2 * CELLS:3 * CELLS].reshape(LAT_ROWS, LAT_COLS, FACE)
    spare_south = perms[3 * CELLS:].reshape(LAT_ROWS, LAT_COLS, FACE)
    across_back = jnp.argsort(across, axis=-1, stable=True).astype(jnp.int32)
    upward_back = jnp.argsort(upward, axis=-1, stable=True).astype(jnp.int32)
    west = jnp.concatenate([spare_west[:, :1], across_back[:, :-1]], axis=1)
    south = jnp.concatenate([spare_south[:1], upward_back[:-1]], axis=0)
    stacked = jnp.stack([west, across, south, upward], axis=2)
    return stacked.reshape(CELLS, 4, FACE).astype(jnp.int32)


def touch_ends(entries, rng, smallest, top_value):
    longest = entries.shape.index(max(entries.shape))
    spots = []
    for shift in (0, 1):
        where = [jax.random.randint(jax.random.fold_in(rng, axis), (), 0, length) for axis, length in enumerate(entries.shape)]
        where[longest] = (where[longest] + shift) % entries.shape[longest]
        spots.append(tuple(where))
    return entries.at[spots[0]].set(smallest).at[spots[1]].set(top_value)


def levels(rng, dims, shards, smallest, top_value):
    def one(dim, blocks):
        heights = jax.random.uniform(jax.random.fold_in(jax.random.fold_in(rng, 6), dim), (blocks,), jnp.float32, smallest / len(shards), top_value / len(shards))
        return jnp.repeat(jnp.exp(heights), dims[dim] // blocks).reshape((-1,) + (1,) * (len(dims) - dim - 1))

    factor_of = one(*shards[0])
    for cut in shards[1:]:
        factor_of = factor_of * one(*cut)
    return factor_of


def normal_values(key, shape, scale, bound, shards=(), held_as=jnp.bfloat16):
    values = scale * jax.random.normal(key, shape, jnp.float32)
    if shards:
        values = values * levels(key, shape, shards, -0.22, 0.18)
    return jnp.clip(values, -bound, bound).astype(held_as)


def setup_inputs(seed: int = 0) -> dict:
    splits = jax.random.split(jax.random.key(seed), 10)
    return {
        "load": normal_values(splits[0], (CELLS, IFACE, RHS), 1.0, 6.0, ((0, 32),), jnp.float32),
        "schur": draw_schur(jax.random.fold_in(splits[9], 71), 0),
        "local_inverse": draw_local_inverse(jax.random.fold_in(splits[9], 71), 0),
        "face_map": draw_face_map(jax.random.fold_in(splits[9], 71), 0),
        "primal_basis": normal_values(splits[4], (CELLS, PRIM, IFACE), (IFACE // 4) ** -0.5, 0.25, ((0, 32),)),
        "primal_index": touch_ends(jax.random.randint(splits[5], (CELLS, PRIM), 0, NCG), jax.random.fold_in(splits[5], 1), 0, NCG - 1).astype(jnp.int32),
        "group_inverse": draw_group_inverse(jax.random.fold_in(splits[9], 71), 0),
        "group_to_coarsest": normal_values(splits[7], (LAT_ROWS, NCG, NQ), NCG ** -0.5, 0.375, ((0, 4), (1, 8)), jnp.float32),
        "coarsest_inverse": draw_coarsest_inverse(jax.random.fold_in(splits[9], 71), 0),
    }


HIGHEST = lax.Precision.HIGHEST


def face_weights():
    rows = jnp.arange(LAT_ROWS)[:, None] + jnp.zeros((1, LAT_COLS), jnp.int32)
    cols = jnp.arange(LAT_COLS)[None, :] + jnp.zeros((LAT_ROWS, 1), jnp.int32)
    exists = jnp.stack([cols > 0, cols < LAT_COLS - 1, rows > 0, rows < LAT_ROWS - 1], axis=2)
    per_face = jnp.where(exists, 0.5, 1.0).astype(jnp.float32)
    return jnp.repeat(per_face, FACE, axis=2).reshape(CELLS, IFACE, 1)


def assemble(values, face_map):
    faces = values.reshape(LAT_ROWS, LAT_COLS, 4, FACE, RHS)
    zero_col = jnp.zeros((LAT_ROWS, 1, FACE, RHS), values.dtype)
    zero_row = jnp.zeros((1, LAT_COLS, FACE, RHS), values.dtype)
    from_west = jnp.concatenate([zero_col, faces[:, :-1, 1]], axis=1)
    from_east = jnp.concatenate([faces[:, 1:, 0], zero_col], axis=1)
    from_south = jnp.concatenate([zero_row, faces[:-1, :, 3]], axis=0)
    from_north = jnp.concatenate([faces[1:, :, 2], zero_row], axis=0)
    received = jnp.stack([from_west, from_east, from_south, from_north], axis=2).reshape(CELLS * 4, FACE, RHS)
    moved = jax.vmap(lambda block, order: block[order])(received, face_map.reshape(CELLS * 4, FACE))
    return values + moved.reshape(CELLS, IFACE, RHS)


def precondition(residual, weight_rows, local_inverse, face_map, primal_basis, primal_index, group_inverse, group_to_coarsest, coarsest_inverse):
    weighted = (residual * weight_rows).astype(jnp.bfloat16)

    def per_cell(items):
        matrix, basis, vector = items
        return (jnp.dot(matrix, vector, preferred_element_type=jnp.float32),
                jnp.dot(basis, vector, preferred_element_type=jnp.float32))

    local_part, primal = lax.map(per_cell, (local_inverse, primal_basis, weighted))
    owners = (jnp.arange(CELLS) // LAT_COLS)[:, None].astype(jnp.int32) * NCG + primal_index.astype(jnp.int32)
    group_coarse = jax.ops.segment_sum(primal.reshape(CELLS * PRIM, RHS), owners.reshape(-1), num_segments=LAT_ROWS * NCG)
    group_coarse = group_coarse.reshape(LAT_ROWS, NCG, RHS)
    coarsest = jnp.einsum('gkq,gkr->qr', group_to_coarsest, group_coarse, precision=HIGHEST)
    coarsest_solution = jnp.dot(coarsest_inverse, coarsest, precision=HIGHEST)
    group_solution = jnp.einsum('gkl,glr->gkr', group_inverse, group_coarse, precision=HIGHEST)
    group_solution = group_solution + jnp.einsum('gkq,qr->gkr', group_to_coarsest, coarsest_solution, precision=HIGHEST)
    picked = group_solution.reshape(LAT_ROWS * NCG, RHS)[owners]
    coarse_part = jnp.einsum('cpi,cpr->cir', primal_basis.astype(jnp.float32), picked, precision=HIGHEST)
    return assemble((local_part + coarse_part) * weight_rows, face_map)


def reference(load, schur, local_inverse, face_map, primal_basis, primal_index, group_inverse, group_to_coarsest, coarsest_inverse):
    weight_rows = face_weights()

    def apply_pre(values):
        return precondition(values, weight_rows, local_inverse, face_map, primal_basis, primal_index, group_inverse, group_to_coarsest, coarsest_inverse)

    rhs_side = assemble(load, face_map)
    solution = jnp.zeros_like(rhs_side)
    residual = rhs_side
    search = apply_pre(residual)
    direction = search
    product = jnp.sum(weight_rows * residual * search, axis=(0, 1))
    for iteration in range(ITERS):
        image_local = lax.map(lambda items: jnp.dot(items[0], items[1].astype(jnp.bfloat16), preferred_element_type=jnp.float32), (schur, direction))
        image = assemble(image_local, face_map)
        curvature = jnp.sum(weight_rows * direction * image, axis=(0, 1))
        alpha = product / curvature
        solution = solution + alpha * direction
        residual = residual - alpha * image
        if iteration + 1 < ITERS:
            search = apply_pre(residual)
            product_next = jnp.sum(weight_rows * residual * search, axis=(0, 1))
            direction = search + (product_next / product) * direction
            product = product_next
    return solution, residual
```

```python
import jax
import jax.numpy as jnp
from jax import lax
from jax.sharding import PartitionSpec as P

HIGHEST = lax.Precision.HIGHEST
EXTRA = 8


def high_dot(a, b):
    return jnp.dot(a, b, precision=HIGHEST)


def pairs(count, odd):
    return [p for i in range(odd, count - 1, 2) for p in ((i, i + 1), (i + 1, i))]


def swap(block, axis, odd):
    return lax.ppermute(block, axis, pairs(lax.axis_size(axis), odd))


def exchange(values):
    face = values.shape[0] // 4
    parts = [values[i * face : (i + 1) * face] for i in range(4)]
    got = [None] * 4
    for axis, low, high in (("grp", 2, 3), ("cell", 0, 1)):
        even = lax.axis_index(axis) % 2 == 0
        first = swap(jnp.where(even, parts[high], parts[low]), axis, 0)
        second = swap(jnp.where(even, parts[low], parts[high]), axis, 1)
        got[high] = jnp.where(even, first, second)
        got[low] = jnp.where(even, second, first)
    return got


def permuted(orders, got):
    out = []
    for i in range(4):
        block = got[i]
        high = block.astype(jnp.bfloat16)
        low = (block - high.astype(jnp.float32)).astype(jnp.bfloat16)
        out.append(
            jnp.dot(orders[i], high, preferred_element_type=jnp.float32)
            + jnp.dot(orders[i], low, preferred_element_type=jnp.float32)
        )
    return jnp.concatenate(out)


def face_weights(ifaces):
    grp_index = lax.axis_index("grp")
    cell_index = lax.axis_index("cell")
    exists = jnp.stack(
        [
            cell_index > 0,
            cell_index < lax.axis_size("cell") - 1,
            grp_index > 0,
            grp_index < lax.axis_size("grp") - 1,
        ]
    )
    per_face = jnp.where(exists, 0.5, 1.0).astype(jnp.float32)
    return jnp.repeat(per_face, ifaces // 4)[:, None]


def body(
    load,
    schur,
    local_inverse,
    face_map,
    primal_basis,
    primal_index,
    group_inverse,
    group_to_coarsest,
    coarsest_inverse,
):
    groups = lax.axis_size("grp")
    cells = lax.axis_size("cell")
    grp_index = lax.axis_index("grp")
    ifaces, columns = load.shape[1:]
    prim = primal_basis.shape[1]
    owned, row_unknowns = group_inverse.shape[1:]
    coarsest_n = coarsest_inverse.shape[0]
    load, schur, local_inverse, basis = load[0], schur[0], local_inverse[0], primal_basis[0]
    weights = face_weights(ifaces)
    face = ifaces // 4
    orders = (face_map[0][:, :, None] == lax.iota(jnp.int32, face)[None, None, :]).astype(
        jnp.bfloat16
    )

    width = row_unknowns + coarsest_n
    index_row = jnp.pad(primal_index.astype(jnp.float32), ((0, 7), (0, width - prim)))
    level = jnp.concatenate(
        [jnp.concatenate([group_inverse[0], group_to_coarsest[0]], axis=1), index_row], axis=0
    )
    level = lax.all_gather(level, "cell", axis=0, tiled=False)
    row_inverse = level[:, :owned, :row_unknowns].reshape(row_unknowns, row_unknowns)
    lifting = level[:, :owned, row_unknowns:].reshape(row_unknowns, coarsest_n)
    row_index = level[:, owned, :prim].reshape(1, cells * prim)
    spread = (row_index == lax.iota(jnp.float32, row_unknowns)[:, None]).astype(jnp.float32)
    own = (
        primal_index[0][:, None] == lax.iota(jnp.int32, row_unknowns)[None, :]
    ).astype(jnp.float32)
    own_map = high_dot(high_dot(own, row_inverse), spread)
    down_map = high_dot(lifting.T, spread)
    up_map = high_dot(high_dot(own, lifting), coarsest_inverse)

    def assembled(values, got):
        return values + permuted(orders, got)

    def weighted(values):
        return (values * weights).astype(jnp.bfloat16)

    def wide(matrix, values):
        return jnp.dot(matrix, values, preferred_element_type=jnp.float32)

    def raised(picked):
        high = picked.astype(jnp.bfloat16)
        low = (picked - high.astype(jnp.float32)).astype(jnp.bfloat16)
        return wide(basis.T, high) + wide(basis.T, low)

    residual = assembled(load, exchange(load))
    half = weighted(residual)
    row_primal = lax.all_gather(wide(basis, half), "cell", axis=0, tiled=True)
    local = wide(local_inverse, half)
    sent = jnp.concatenate([high_dot(down_map, row_primal), up_map.reshape(-1, columns)])
    sent = lax.all_gather(sent, "grp", axis=0, tiled=False)
    coarsest = jnp.sum(sent[:, :coarsest_n], axis=0)
    up_all = sent[:, coarsest_n:].reshape(groups * prim, coarsest_n)
    picked = high_dot(own_map, row_primal) + high_dot(up_map, coarsest)

    block = prim + EXTRA
    picks = high_dot(up_all, down_map).reshape(groups, prim, cells, prim)
    mine = (lax.iota(jnp.int32, groups) == grp_index).astype(jnp.float32)[:, None, None, None]
    picks = picks + mine * own_map.reshape(1, prim, cells, prim)
    chain = jnp.concatenate(
        [
            jnp.pad(picks, ((0, 0), (0, 0), (0, 0), (0, EXTRA))),
            jnp.broadcast_to(
                jnp.pad(jnp.eye(EXTRA, dtype=jnp.float32), ((0, 0), (prim, 0)))[None, :, None, :],
                (groups, EXTRA, cells, block),
            ),
        ],
        axis=1,
    ).reshape(groups * block, cells * block)

    shared = (local + raised(picked)) * weights
    search = assembled(shared, exchange(shared))
    image_own = wide(schur, search.astype(jnp.bfloat16))
    sums = jnp.stack(
        [jnp.sum(weights * residual * search, axis=0), jnp.sum(search * image_own, axis=0)]
    )
    image = assembled(image_own, exchange(image_own))
    primal = wide(basis, weighted(image))
    sent = jnp.concatenate([primal, jnp.pad(sums, ((0, EXTRA - 2), (0, 0)))])
    sent = lax.all_gather(sent, "cell", axis=0, tiled=True)
    sent = lax.all_to_all(high_dot(chain, sent), "grp", 0, 0, tiled=True)
    sent = jnp.sum(sent.reshape(groups, block, columns), axis=0)
    product, curvature = sent[prim], sent[prim + 1]
    alpha = product / curvature
    residual = residual - alpha * image
    shared = (wide(local_inverse, weighted(residual)) + raised(picked - alpha * sent[:prim])) * weights
    second = assembled(shared, exchange(shared))
    second_own = wide(schur, second.astype(jnp.bfloat16))
    sums = jnp.stack(
        [
            jnp.sum(weights * residual * second, axis=0),
            jnp.sum(second * second_own, axis=0),
            jnp.sum(second * image_own, axis=0),
        ]
    )
    sums = jnp.pad(sums, ((0, EXTRA - 3), (0, 0)))
    sums = jnp.broadcast_to(sums[None], (groups * cells, EXTRA, columns))
    got = exchange(second_own)
    sums = lax.all_to_all(sums, ("grp", "cell"), 0, 0, tiled=True)
    sums = jnp.sum(sums, axis=0)
    beta = sums[0] / product
    alpha_next = sums[0] / (sums[1] + beta * (2.0 * sums[2] + beta * curvature))
    direction = second + beta * search
    image = assembled(second_own, got) + beta * image
    return (
        (alpha * search + alpha_next * direction)[None],
        (residual - alpha_next * image)[None],
    )


def solution(mesh):
    split = ("grp", "cell")
    placed = (
        P(split, None, None),
        P(split, None, None),
        P(split, None, None),
        P(split, None, None),
        P(split, None, None),
        P(split, None),
        P("grp", "cell", None),
        P("grp", "cell", None),
        P(),
    )
    return jax.shard_map(
        body,
        mesh=mesh,
        in_specs=placed,
        out_specs=(P(split, None, None), P(split, None, None)),
        check_vma=False,
    )
```

```python
import functools

import jax
import jax.numpy as jnp
from jax import lax
from jax.experimental import pallas as pl
from jax.experimental.pallas import tpu as pltpu
from jax.sharding import PartitionSpec as P

HIGHEST = lax.Precision.HIGHEST
EXTRA = 8
F32, BF16 = jnp.float32, jnp.bfloat16
ANY = pl.BlockSpec(memory_space=pl.ANY)
VMEM = pl.BlockSpec(memory_space=pltpu.VMEM)


def high_dot(a, b):
    return jnp.dot(a, b, precision=HIGHEST)


def wide(a, b):
    return jnp.dot(a, b, preferred_element_type=F32)


def pairs(count, odd):
    return [p for i in range(odd, count - 1, 2) for p in ((i, i + 1), (i + 1, i))]


def exchange(parts):
    return [
        lax.ppermute(part, axis, pairs(lax.axis_size(axis), odd))
        for part, (axis, odd) in zip(parts, (("grp", 0), ("grp", 1), ("cell", 0), ("cell", 1)))
    ]


def slots():
    faces, weights = [], []
    for axis, low in (("grp", 2), ("cell", 0)):
        index, count = lax.axis_index(axis), lax.axis_size(axis)
        odd = lax.rem(index, 2)
        for up in (1 - odd, odd):
            there = jnp.where(up == 1, index < count - 1, index > 0)
            faces.append(low + up)
            weights.append(jnp.where(there, 0.5, 1.0).astype(F32))
    return faces, weights


class Copies:
    def __init__(self, sems):
        self.sems, self.used = sems, 0

    def start(self, source, target):
        copy = pltpu.make_async_copy(source, target, self.sems.at[self.used])
        self.used += 1
        copy.start()
        return copy


def rows_of(face, size):
    return pl.ds(pl.multiple_of(face * size, size), size)


def split(values):
    high = values.astype(BF16)
    low = (values - high.astype(F32)).astype(BF16)
    return jnp.concatenate([high, low], axis=1)


def exact(matrix, values):
    both = wide(matrix, split(values))
    half = both.shape[1] // 2
    return both[:, :half] + both[:, half:]


def column_sums(values):
    return jnp.sum(values, axis=0, keepdims=True)


def call(kernel, inputs, specs, outs, out_specs, scratch, copies, flops):
    moved = sum(a.size * a.dtype.itemsize for a in inputs)
    return pl.pallas_call(
        kernel,
        out_shape=outs,
        in_specs=specs,
        out_specs=out_specs,
        scratch_shapes=[*scratch, pltpu.SemaphoreType.DMA((copies,))],
        compiler_params=pltpu.CompilerParams(vmem_limit_bytes=40 * 2**20),
        cost_estimate=pl.CostEstimate(flops=flops, bytes_accessed=moved, transcendentals=0),
    )(*inputs)


def split_faces(load):
    size, columns = load.shape[0] // 4, load.shape[1]

    def kernel(load_ref, *refs):
        outs, sems = refs[:4], refs[4]
        faces, _ = slots()
        moves = Copies(sems)
        for copy in [moves.start(load_ref.at[rows_of(faces[s], size)], outs[s]) for s in range(4)]:
            copy.wait()

    return call(
        kernel,
        [load],
        [ANY],
        [jax.ShapeDtypeStruct((size, columns), F32)] * 4,
        [ANY] * 4,
        [],
        4,
        0,
    )


def gather_primal(own, got, orders, basis, sums):
    size, columns = own[0].shape
    prim = basis.shape[0]
    whole = (4 * size, columns)

    def kernel(*refs):
        own_refs, got_refs, (order_ref, basis_ref, sums_ref) = refs[:4], refs[4:8], refs[8:11]
        full_ref, half_ref, sent_ref = refs[11:14]
        own_buf, got_buf, order_buf, full_buf, half_buf, sems = refs[14:]
        faces, weights = slots()
        moves = Copies(sems)
        loads = [
            (
                moves.start(got_refs[s], got_buf.at[s]),
                moves.start(order_ref.at[faces[s]], order_buf.at[s]),
                moves.start(own_refs[s], own_buf.at[s]),
            )
            for s in range(4)
        ]
        stores = []
        for s in range(4):
            for copy in loads[s]:
                copy.wait()
            full = own_buf[s] + exact(order_buf[s], got_buf[s])
            rows = rows_of(faces[s], size)
            full_buf[s] = full
            stores.append(moves.start(full_buf.at[s], full_ref.at[rows]))
            half_buf[rows, :] = (full * weights[s]).astype(BF16)
        stores.append(moves.start(half_buf, half_ref))
        sent_ref[:prim, :] = wide(basis_ref[...], half_buf[...])
        sent_ref[prim:, :] = sums_ref[...]
        for copy in stores:
            copy.wait()

    return call(
        kernel,
        [*own, *got, orders, basis, sums],
        [ANY] * 9 + [VMEM] * 2,
        [
            jax.ShapeDtypeStruct(whole, F32),
            jax.ShapeDtypeStruct(whole, BF16),
            jax.ShapeDtypeStruct((prim + EXTRA, columns), F32),
        ],
        [ANY, ANY, VMEM],
        [
            pltpu.VMEM((4, size, columns), F32),
            pltpu.VMEM((4, size, columns), F32),
            pltpu.VMEM((4, size, size), BF16),
            pltpu.VMEM((4, size, columns), F32),
            pltpu.VMEM(whole, BF16),
        ],
        17,
        2 * 4 * size * columns * (2 * size + prim),
    )


def solve_first(half, matrix, lift, picked):
    n, columns = half.shape
    size = n // 4

    def kernel(half_ref, matrix_ref, lift_ref, picked_ref, *refs):
        outs, (half_buf, matrix_buf, out_buf, sems) = refs[:4], refs[4:]
        faces, weights = slots()
        moves = Copies(sems)
        first = moves.start(half_ref, half_buf)
        loads = [
            moves.start(matrix_ref.at[rows_of(faces[s], size)], matrix_buf.at[s]) for s in range(4)
        ]
        picked = split(picked_ref[...])
        first.wait()
        stores = []
        for s in range(4):
            raised = wide(lift_ref[rows_of(faces[s], size), :], picked)
            raised = raised[:, :columns] + raised[:, columns:]
            loads[s].wait()
            out_buf[s] = (wide(matrix_buf[s], half_buf[...]) + raised) * weights[s]
            stores.append(moves.start(out_buf.at[s], outs[s]))
        for copy in stores:
            copy.wait()

    return call(
        kernel,
        [half, matrix, lift, picked],
        [ANY, ANY, VMEM, VMEM],
        [jax.ShapeDtypeStruct((size, columns), F32)] * 4,
        [ANY] * 4,
        [
            pltpu.VMEM((n, columns), BF16),
            pltpu.VMEM((4, size, n), BF16),
            pltpu.VMEM((4, size, columns), F32),
        ],
        9,
        2 * n * columns * n,
    )


def solve_second(residual, image, matrix, lift, picked, sent):
    n, columns = residual.shape
    size = n // 4
    prim = picked.shape[0]

    def kernel(residual_ref, image_ref, matrix_ref, lift_ref, picked_ref, sent_ref, *refs):
        outs, next_ref, total_ref = refs[:4], refs[4], refs[5]
        res_buf, image_buf, half_buf, matrix_buf, out_buf, sems = refs[6:]
        faces, weights = slots()
        moves = Copies(sems)
        early = []
        for s in range(4):
            rows = rows_of(faces[s], size)
            early.append(
                (
                    moves.start(residual_ref.at[rows], res_buf.at[s]),
                    moves.start(image_ref.at[rows], image_buf.at[s]),
                )
            )
        loads = [
            moves.start(matrix_ref.at[rows_of(faces[s], size)], matrix_buf.at[s]) for s in range(4)
        ]
        total = jnp.sum(sent_ref[...], axis=0)
        total_ref[...] = total[prim:]
        alpha = total[prim : prim + 1] / total[prim + 1 : prim + 2]
        picked = split(picked_ref[...] - alpha * total[:prim])
        stores = []
        for s in range(4):
            for copy in early[s]:
                copy.wait()
            rows = rows_of(faces[s], size)
            res = res_buf[s] - alpha * image_buf[s]
            res_buf[s] = res
            stores.append(moves.start(res_buf.at[s], next_ref.at[rows]))
            half_buf[rows, :] = (res * weights[s]).astype(BF16)
        for s in range(4):
            raised = wide(lift_ref[rows_of(faces[s], size), :], picked)
            raised = raised[:, :columns] + raised[:, columns:]
            loads[s].wait()
            out_buf[s] = (wide(matrix_buf[s], half_buf[...]) + raised) * weights[s]
            stores.append(moves.start(out_buf.at[s], outs[s]))
        for copy in stores:
            copy.wait()

    return call(
        kernel,
        [residual, image, matrix, lift, picked, sent],
        [ANY, ANY, ANY, VMEM, VMEM, VMEM],
        [jax.ShapeDtypeStruct((size, columns), F32)] * 4
        + [
            jax.ShapeDtypeStruct((n, columns), F32),
            jax.ShapeDtypeStruct((sent.shape[1] - prim, columns), F32),
        ],
        [ANY] * 5 + [VMEM],
        [
            pltpu.VMEM((4, size, columns), F32),
            pltpu.VMEM((4, size, columns), F32),
            pltpu.VMEM((n, columns), BF16),
            pltpu.VMEM((4, size, n), BF16),
            pltpu.VMEM((4, size, columns), F32),
        ],
        20,
        2 * n * columns * n,
    )


def image_of(own, got, orders, matrix, residual, past):
    size, columns = own[0].shape
    n = 4 * size
    extra = len(past)

    def kernel(*refs):
        own_refs, got_refs, (order_ref, matrix_ref, residual_ref) = refs[:4], refs[4:8], refs[8:11]
        past_refs, refs = refs[11 : 11 + extra], refs[11 + extra :]
        search_ref, outs, sums_ref = refs[0], refs[1:5], refs[5]
        own_buf, got_buf, order_buf, res_buf, half_buf, matrix_buf, out_buf, past_buf, sems = refs[6:]
        faces, weights = slots()
        moves = Copies(sems)
        early = [
            (
                moves.start(got_refs[s], got_buf.at[s]),
                moves.start(order_ref.at[faces[s]], order_buf.at[s]),
                moves.start(own_refs[s], own_buf.at[s]),
            )
            for s in range(4)
        ]
        late = []
        for s in range(4):
            rows = rows_of(faces[s], size)
            late.append([moves.start(matrix_ref.at[rows], matrix_buf.at[s])])
        for s in range(4):
            late[s].append(moves.start(residual_ref.at[rows_of(faces[s], size)], res_buf.at[s]))
            if extra:
                late[s].append(moves.start(past_refs[s], past_buf.at[s]))
        stores = []
        for s in range(4):
            for copy in early[s]:
                copy.wait()
            search = own_buf[s] + exact(order_buf[s], got_buf[s])
            rows = rows_of(faces[s], size)
            own_buf[s] = search
            stores.append(moves.start(own_buf.at[s], search_ref.at[rows]))
            half_buf[rows, :] = search.astype(BF16)
        sums = [jnp.zeros((1, columns), F32) for _ in range(3)]
        for s in range(4):
            for copy in late[s]:
                copy.wait()
            image = wide(matrix_buf[s], half_buf[...])
            out_buf[s] = image
            stores.append(moves.start(out_buf.at[s], outs[s]))
            search = own_buf[s]
            sums[0] += weights[s] * column_sums(res_buf[s] * search)
            sums[1] += column_sums(search * image)
            if extra:
                sums[2] += column_sums(search * past_buf[s])
        sums_ref[...] = jnp.concatenate(sums + [jnp.zeros((EXTRA - 3, columns), F32)], axis=0)
        for copy in stores:
            copy.wait()

    return call(
        kernel,
        [*own, *got, orders, matrix, residual, *past],
        [ANY] * (11 + extra),
        [jax.ShapeDtypeStruct((n, columns), F32)]
        + [jax.ShapeDtypeStruct((size, columns), F32)] * 4
        + [jax.ShapeDtypeStruct((EXTRA, columns), F32)],
        [ANY] * 5 + [VMEM],
        [
            pltpu.VMEM((4, size, columns), F32),
            pltpu.VMEM((4, size, columns), F32),
            pltpu.VMEM((4, size, size), BF16),
            pltpu.VMEM((4, size, columns), F32),
            pltpu.VMEM((n, columns), BF16),
            pltpu.VMEM((4, size, n), BF16),
            pltpu.VMEM((4, size, columns), F32),
            pltpu.VMEM((4, size, columns) if extra else (1, 8, 128), F32),
        ],
        32,
        2 * n * columns * (n + 2 * size),
    )


def finish(own, got, orders, search, second, residual, image, total, sums):
    size, columns = own[0].shape
    n = 4 * size

    def kernel(*refs):
        own_refs, got_refs, order_ref = refs[:4], refs[4:8], refs[8]
        whole_refs, (total_ref, sums_ref) = refs[9:13], refs[13:15]
        out_refs = refs[15:17]
        own_buf, got_buf, order_buf, whole_buf, sems = refs[17:]
        faces, _ = slots()
        moves = Copies(sems)
        loads = []
        for s in range(4):
            rows = rows_of(faces[s], size)
            loads.append(
                [
                    moves.start(got_refs[s], got_buf.at[s]),
                    moves.start(order_ref.at[faces[s]], order_buf.at[s]),
                    moves.start(own_refs[s], own_buf.at[s]),
                ]
                + [moves.start(whole_refs[k].at[rows], whole_buf.at[k, s]) for k in range(4)]
            )
        product, curvature = total_ref[0:1, :], total_ref[1:2, :]
        sums = jnp.sum(sums_ref[...], axis=0)
        alpha = product / curvature
        beta = sums[0:1] / product
        alpha_next = sums[0:1] / (sums[1:2] + beta * (2.0 * sums[2:3] + beta * curvature))
        stores = []
        for s in range(4):
            for copy in loads[s]:
                copy.wait()
            rows = rows_of(faces[s], size)
            image = own_buf[s] + exact(order_buf[s], got_buf[s]) + beta * whole_buf[3, s]
            own_buf[s] = whole_buf[2, s] - alpha_next * image
            search = whole_buf[0, s]
            got_buf[s] = alpha * search + alpha_next * (whole_buf[1, s] + beta * search)
            stores.append(moves.start(got_buf.at[s], out_refs[0].at[rows]))
            stores.append(moves.start(own_buf.at[s], out_refs[1].at[rows]))
        for copy in stores:
            copy.wait()

    return call(
        kernel,
        [*own, *got, orders, search, second, residual, image, total, sums],
        [ANY] * 13 + [VMEM] * 2,
        [jax.ShapeDtypeStruct((n, columns), F32)] * 2,
        [ANY] * 2,
        [
            pltpu.VMEM((4, size, columns), F32),
            pltpu.VMEM((4, size, columns), F32),
            pltpu.VMEM((4, size, size), BF16),
            pltpu.VMEM((4, 4, size, columns), F32),
        ],
        36,
        2 * n * columns * 2 * size,
    )


def body(
    load,
    schur,
    local_inverse,
    face_map,
    primal_basis,
    primal_index,
    group_inverse,
    group_to_coarsest,
    coarsest_inverse,
):
    groups = lax.axis_size("grp")
    cells = lax.axis_size("cell")
    grp_index = lax.axis_index("grp")
    ifaces, columns = load.shape[1:]
    prim = primal_basis.shape[1]
    owned, row_unknowns = group_inverse.shape[1:]
    coarsest_n = coarsest_inverse.shape[0]
    schur, local_inverse, basis = schur[0], local_inverse[0], primal_basis[0]
    face = ifaces // 4
    block = prim + EXTRA

    own = split_faces(load[0])
    got = exchange(own)
    orders = (face_map[0][:, :, None] == lax.iota(jnp.int32, face)[None, None, :]).astype(BF16)
    lift = basis.T

    width = row_unknowns + coarsest_n
    index_row = jnp.pad(primal_index.astype(F32), ((0, 7), (0, width - prim)))
    level = jnp.concatenate(
        [jnp.concatenate([group_inverse[0], group_to_coarsest[0]], axis=1), index_row], axis=0
    )
    level = lax.all_gather(level, "cell", axis=0, tiled=False)
    row_inverse = level[:, :owned, :row_unknowns].reshape(row_unknowns, row_unknowns)
    lifting = level[:, :owned, row_unknowns:].reshape(row_unknowns, coarsest_n)
    row_index = level[:, owned, :prim]
    row_index = jnp.pad(row_index, ((0, 0), (0, EXTRA)), constant_values=-1.0)
    row_index = row_index.reshape(1, cells * block)
    spread = (row_index == lax.iota(F32, row_unknowns)[:, None]).astype(F32)
    picks = (primal_index[0][:, None] == lax.iota(jnp.int32, row_unknowns)[None, :]).astype(F32)
    own_map = high_dot(high_dot(picks, row_inverse), spread)
    down_map = high_dot(lifting.T, spread)
    up_map = high_dot(high_dot(picks, lifting), coarsest_inverse)

    residual, half, sent = gather_primal(own, got, orders, basis, jnp.zeros((EXTRA, columns), F32))
    row_primal = lax.all_gather(sent, "cell", axis=0, tiled=True)
    sent = jnp.concatenate([high_dot(down_map, row_primal), up_map.reshape(-1, columns)])
    sent = lax.all_gather(sent, "grp", axis=0, tiled=False)
    coarsest = jnp.sum(sent[:, :coarsest_n], axis=0)
    up_all = sent[:, coarsest_n:].reshape(groups * prim, coarsest_n)
    picked = high_dot(own_map, row_primal) + high_dot(up_map, coarsest)

    mine = (lax.iota(jnp.int32, groups) == grp_index).astype(F32)[:, None, None]
    chain = high_dot(up_all, down_map).reshape(groups, prim, cells * block) + mine * own_map[None]
    sums_map = jnp.tile(jnp.eye(EXTRA, block, prim, dtype=F32), (1, cells))
    chain = jnp.concatenate(
        [chain, jnp.broadcast_to(sums_map[None], (groups,) + sums_map.shape)], axis=1
    ).reshape(groups * block, cells * block)

    own = solve_first(half, local_inverse, lift, picked)
    search, *own, sums = image_of(own, exchange(own), orders, schur, residual, ())
    image, _, sent = gather_primal(own, exchange(own), orders, basis, sums)
    sent = lax.all_gather(sent, "cell", axis=0, tiled=True)
    sent = lax.all_to_all(high_dot(chain, sent), "grp", 0, 0, tiled=True)
    *shared, residual, total = solve_second(
        residual, image, local_inverse, lift, picked, sent.reshape(groups, block, columns)
    )
    second, *own, sums = image_of(shared, exchange(shared), orders, schur, residual, own)
    sums = jnp.broadcast_to(sums[None], (groups * cells, EXTRA, columns))
    got = exchange(own)
    sums = lax.all_to_all(sums, ("grp", "cell"), 0, 0, tiled=True)
    result, residual = finish(own, got, orders, search, second, residual, image, total, sums)
    return result[None], residual[None]


def solution(mesh):
    split_axes = ("grp", "cell")
    placed = (
        P(split_axes, None, None),
        P(split_axes, None, None),
        P(split_axes, None, None),
        P(split_axes, None, None),
        P(split_axes, None, None),
        P(split_axes, None),
        P("grp", "cell", None),
        P("grp", "cell", None),
        P(),
    )
    return jax.shard_map(
        body,
        mesh=mesh,
        in_specs=placed,
        out_specs=(P(split_axes, None, None), P(split_axes, None, None)),
        check_vma=False,
    )
```

```python
import functools

import jax
import jax.numpy as jnp
from jax import lax
from jax.experimental import pallas as pl
from jax.experimental.pallas import tpu as pltpu
from jax.sharding import PartitionSpec as P

HIGHEST = lax.Precision.HIGHEST
EXTRA = 8
F32, BF16 = jnp.float32, jnp.bfloat16
ANY = pl.BlockSpec(memory_space=pl.ANY)
VMEM = pl.BlockSpec(memory_space=pltpu.VMEM)


def high_dot(a, b):
    return jnp.dot(a, b, precision=HIGHEST)


def wide(a, b):
    return jnp.dot(a, b, preferred_element_type=F32)


def pairs(count, odd):
    return [p for i in range(odd, count - 1, 2) for p in ((i, i + 1), (i + 1, i))]


def exchange(parts):
    return [
        lax.ppermute(part, axis, pairs(lax.axis_size(axis), odd))
        for part, (axis, odd) in zip(parts, (("grp", 0), ("grp", 1), ("cell", 0), ("cell", 1)))
    ]


def slots():
    faces, weights = [], []
    for axis, low in (("grp", 2), ("cell", 0)):
        index, count = lax.axis_index(axis), lax.axis_size(axis)
        odd = lax.rem(index, 2)
        for up in (1 - odd, odd):
            there = jnp.where(up == 1, index < count - 1, index > 0)
            faces.append(low + up)
            weights.append(jnp.where(there, 0.5, 1.0).astype(F32))
    return faces, weights


def rows_of(face, size):
    return pl.ds(pl.multiple_of(face * size, size), size)


def split(values):
    high = values.astype(BF16)
    low = (values - high.astype(F32)).astype(BF16)
    return jnp.concatenate([high, low], axis=1)


def exact(matrix, values):
    both = wide(matrix, split(values))
    half = both.shape[1] // 2
    return both[:, :half] + both[:, half:]


def column_sums(values):
    return jnp.sum(values, axis=0, keepdims=True)


def stacked(values, pieces):
    width = values.shape[1] // pieces
    return jnp.concatenate([values[:, k * width : (k + 1) * width] for k in range(pieces)], axis=0)


def beside(values, pieces):
    height = values.shape[0] // pieces
    return jnp.concatenate(
        [values[k * height : (k + 1) * height] for k in range(pieces)], axis=1
    )


def call(kernel, inputs, specs, outs, out_specs, scratch, flops):
    moved = sum(a.size * a.dtype.itemsize for a in inputs)
    return pl.pallas_call(
        kernel,
        out_shape=outs,
        in_specs=specs,
        out_specs=out_specs,
        scratch_shapes=scratch,
        compiler_params=pltpu.CompilerParams(vmem_limit_bytes=24 * 2**20),
        cost_estimate=pl.CostEstimate(flops=flops, bytes_accessed=moved // 8, transcendentals=0),
    )(*inputs)


def shape(*dims):
    return jax.ShapeDtypeStruct(dims, F32)


def split_faces(load):
    size, columns = load.shape[0] // 4, load.shape[1]

    def kernel(load_ref, *refs):
        outs, sems = refs[:4], refs[4]
        faces, _ = slots()
        copies = [
            pltpu.make_async_copy(load_ref.at[rows_of(faces[s], size)], outs[s], sems.at[s])
            for s in range(4)
        ]
        for copy in copies:
            copy.start()
        for copy in copies:
            copy.wait()

    return call(
        kernel,
        [load],
        [ANY],
        [shape(size, columns)] * 4,
        [VMEM] * 4,
        [pltpu.SemaphoreType.DMA((4,))],
        0,
    )


def gather_primal(own, got, orders, basis, tail):
    size, columns = own[0].shape
    prim = basis.shape[0]
    whole = (4 * size, columns)

    def kernel(*refs):
        own_refs, got_refs, (order_ref, basis_ref, tail_ref) = refs[:4], refs[4:8], refs[8:11]
        full_ref, half_ref, sent_ref = refs[11:]
        faces, weights = slots()
        sent_ref[prim:, :] = tail_ref[...]
        for s in range(4):
            full = own_refs[s][...] + exact(order_ref[faces[s]], got_refs[s][...])
            full_ref[s] = full
            half_ref[rows_of(faces[s], size), :] = (full * weights[s]).astype(BF16)
        sent_ref[:prim, :] = wide(basis_ref[...], half_ref[...])

    return call(
        kernel,
        [*own, *got, orders, basis, tail],
        [VMEM] * 11,
        [
            shape(4, size, columns),
            jax.ShapeDtypeStruct(whole, BF16),
            shape(prim + tail.shape[0], columns),
        ],
        [VMEM] * 3,
        [],
        2 * 4 * size * columns * (2 * size + prim),
    )


class Level:
    def __init__(self, prim, owned, unknowns, coarsest, columns):
        self.prim, self.owned, self.unknowns, self.coarsest = prim, owned, unknowns, coarsest
        self.inverse_pieces, self.lift_pieces = unknowns // columns, columns // coarsest
        self.at_inverse = prim
        self.at_lift = self.at_inverse + owned * self.inverse_pieces
        self.at_index = self.at_lift + owned // self.lift_pieces
        self.columns = columns

    def tail(self, inverse, lift, index):
        index = jnp.pad(index.astype(F32), ((0, 7), (0, self.columns - self.prim)))
        return jnp.concatenate(
            [stacked(inverse, self.inverse_pieces), beside(lift, self.lift_pieces), index], axis=0
        )

    def read(self, ref, cells):
        inverse, lift, index = [], [], []
        for cell in range(cells):
            inverse.append(beside(ref[cell, self.at_inverse : self.at_lift, :], self.inverse_pieces))
            lift.append(stacked(ref[cell, self.at_lift : self.at_index, :], self.lift_pieces))
            index.append(ref[cell, self.at_index : self.at_index + 1, : self.prim])
        inverse, lift = jnp.concatenate(inverse, axis=0), jnp.concatenate(lift, axis=0)
        index = jnp.concatenate(index, axis=1).astype(jnp.int32)
        rows = lax.broadcasted_iota(jnp.int32, (self.unknowns, cells * self.prim), 0)
        return inverse, lift, (rows == index).astype(F32)

    def primal(self, ref, cells):
        return jnp.concatenate([ref[cell, : self.prim, :] for cell in range(cells)], axis=0)

    def picks(self, ref):
        columns = lax.broadcasted_iota(jnp.int32, (self.prim, self.unknowns), 1)
        return (columns == ref[...]).astype(F32)


def lower_first(level, gathered, index, coarsest_inverse):
    cells, _, columns = gathered.shape

    def kernel(gathered_ref, index_ref, coarsest_ref, sent_ref, own_ref, up_ref):
        inverse, lift, spread = level.read(gathered_ref, cells)
        picks = level.picks(index_ref)
        coarse = high_dot(spread, level.primal(gathered_ref, cells))
        own_ref[...] = high_dot(high_dot(picks, inverse), coarse)
        up = high_dot(high_dot(picks, lift), coarsest_ref[...])
        up_ref[...] = up
        sent_ref[: level.coarsest, :] = high_dot(lift.T, coarse)
        sent_ref[level.coarsest :, :] = beside(up, level.lift_pieces)

    return call(
        kernel,
        [gathered, index, coarsest_inverse],
        [VMEM] * 3,
        [
            shape(level.coarsest + level.prim // level.lift_pieces, columns),
            shape(level.prim, columns),
            shape(level.prim, level.coarsest),
        ],
        [VMEM] * 3,
        [],
        0,
    )


def lower_second(level, gathered, index, ups, again):
    cells, block, columns = again.shape
    groups = ups.shape[0]

    def kernel(gathered_ref, index_ref, ups_ref, again_ref, sent_ref):
        inverse, lift, spread = level.read(gathered_ref, cells)
        picks = level.picks(index_ref)
        coarse = high_dot(spread, level.primal(again_ref, cells))
        own = high_dot(high_dot(picks, inverse), coarse)
        lowered = high_dot(lift.T, coarse)
        sums = again_ref[0, level.prim :, :]
        for cell in range(1, cells):
            sums = sums + again_ref[cell, level.prim :, :]
        mine = lax.axis_index("grp")
        for row in range(groups):
            up = stacked(ups_ref[row, level.coarsest :, :], level.lift_pieces)
            sent_ref[row, : level.prim, :] = high_dot(up, lowered) + jnp.where(
                mine == row, own, jnp.zeros_like(own)
            )
            sent_ref[row, level.prim :, :] = sums

    return call(
        kernel,
        [gathered, index, ups, again],
        [VMEM] * 4,
        shape(groups, block, columns),
        VMEM,
        [],
        0,
    )


def solve_first(half, matrix, lift, own, up, sent):
    n, columns = half.shape
    size = n // 4
    prim, coarsest_n = up.shape

    def kernel(half_ref, matrix_ref, lift_ref, own_ref, up_ref, sent_ref, *refs):
        outs, picked_ref = refs[:4], refs[4]
        faces, weights = slots()
        coarsest = jnp.sum(sent_ref[:, :coarsest_n, :], axis=0)
        picked = own_ref[...] + high_dot(up_ref[...], coarsest)
        picked_ref[...] = picked
        picked = split(picked)
        for s in range(4):
            rows = rows_of(faces[s], size)
            raised = wide(lift_ref[rows, :], picked)
            raised = raised[:, :columns] + raised[:, columns:]
            outs[s][...] = (wide(matrix_ref[rows, :], half_ref[...]) + raised) * weights[s]

    return call(
        kernel,
        [half, matrix, lift, own, up, sent],
        [VMEM] * 6,
        [shape(size, columns)] * 4 + [shape(prim, columns)],
        [VMEM] * 5,
        [],
        2 * n * columns * n,
    )


def solve_second(residual, image, matrix, lift, picked, sent):
    _, size, columns = residual.shape
    n = 4 * size
    prim = picked.shape[0]

    def kernel(residual_ref, image_ref, matrix_ref, lift_ref, picked_ref, sent_ref, *refs):
        outs, next_ref, total_ref, half_ref = refs[:4], refs[4], refs[5], refs[6]
        faces, weights = slots()
        total = jnp.sum(sent_ref[...], axis=0)
        total_ref[...] = total[prim:]
        alpha = total[prim : prim + 1] / total[prim + 1 : prim + 2]
        picked = split(picked_ref[...] - alpha * total[:prim])
        for s in range(4):
            res = residual_ref[s] - alpha * image_ref[s]
            next_ref[s] = res
            half_ref[rows_of(faces[s], size), :] = (res * weights[s]).astype(BF16)
        for s in range(4):
            rows = rows_of(faces[s], size)
            raised = wide(lift_ref[rows, :], picked)
            raised = raised[:, :columns] + raised[:, columns:]
            outs[s][...] = (wide(matrix_ref[rows, :], half_ref[...]) + raised) * weights[s]

    return call(
        kernel,
        [residual, image, matrix, lift, picked, sent],
        [VMEM] * 6,
        [shape(size, columns)] * 4
        + [shape(4, size, columns), shape(sent.shape[1] - prim, columns)],
        [VMEM] * 6,
        [pltpu.VMEM((n, columns), BF16)],
        2 * n * columns * n,
    )


def image_of(own, got, orders, matrix, residual, past):
    size, columns = own[0].shape
    n = 4 * size
    extra = len(past)

    def kernel(*refs):
        own_refs, got_refs, (order_ref, matrix_ref, residual_ref) = refs[:4], refs[4:8], refs[8:11]
        past_refs, refs = refs[11 : 11 + extra], refs[11 + extra :]
        search_ref, outs, sums_ref, half_ref = refs[0], refs[1:5], refs[5], refs[6]
        faces, weights = slots()
        for s in range(4):
            search = own_refs[s][...] + exact(order_ref[faces[s]], got_refs[s][...])
            search_ref[s] = search
            half_ref[rows_of(faces[s], size), :] = search.astype(BF16)
        sums = [jnp.zeros((1, columns), F32) for _ in range(3)]
        for s in range(4):
            image = wide(matrix_ref[rows_of(faces[s], size), :], half_ref[...])
            outs[s][...] = image
            search = search_ref[s]
            sums[0] += weights[s] * column_sums(residual_ref[s] * search)
            sums[1] += column_sums(search * image)
            if extra:
                sums[2] += column_sums(search * past_refs[s][...])
        sums_ref[...] = jnp.concatenate(sums + [jnp.zeros((EXTRA - 3, columns), F32)], axis=0)

    return call(
        kernel,
        [*own, *got, orders, matrix, residual, *past],
        [VMEM] * (11 + extra),
        [shape(4, size, columns)] + [shape(size, columns)] * 4 + [shape(EXTRA, columns)],
        [VMEM] * 6,
        [pltpu.VMEM((n, columns), BF16)],
        2 * n * columns * (n + 2 * size),
    )


def finish(own, got, orders, search, second, residual, image, total, sums):
    size, columns = own[0].shape
    n = 4 * size

    def kernel(*refs):
        own_refs, got_refs, order_ref = refs[:4], refs[4:8], refs[8]
        search_ref, second_ref, residual_ref, image_ref, total_ref, sums_ref = refs[9:15]
        out_refs, (solution_buf, residual_buf, sems) = refs[15:17], refs[17:]
        faces, _ = slots()
        product, curvature = total_ref[0:1, :], total_ref[1:2, :]
        sums = jnp.sum(sums_ref[...], axis=0)
        alpha = product / curvature
        beta = sums[0:1] / product
        alpha_next = sums[0:1] / (sums[1:2] + beta * (2.0 * sums[2:3] + beta * curvature))
        stores = []
        for s in range(4):
            rows = rows_of(faces[s], size)
            image = own_refs[s][...] + exact(order_ref[faces[s]], got_refs[s][...])
            residual_buf[s] = residual_ref[s] - alpha_next * (image + beta * image_ref[s])
            search = search_ref[s]
            solution_buf[s] = alpha * search + alpha_next * (second_ref[s] + beta * search)
            for k, buf in enumerate((solution_buf, residual_buf)):
                copy = pltpu.make_async_copy(buf.at[s], out_refs[k].at[rows], sems.at[2 * s + k])
                copy.start()
                stores.append(copy)
        for copy in stores:
            copy.wait()

    return call(
        kernel,
        [*own, *got, orders, search, second, residual, image, total, sums],
        [VMEM] * 15,
        [shape(n, columns)] * 2,
        [ANY] * 2,
        [
            pltpu.VMEM((4, size, columns), F32),
            pltpu.VMEM((4, size, columns), F32),
            pltpu.SemaphoreType.DMA((8,)),
        ],
        2 * n * columns * 2 * size,
    )


def body(
    load,
    schur,
    local_inverse,
    face_map,
    primal_basis,
    primal_index,
    group_inverse,
    group_to_coarsest,
    coarsest_inverse,
):
    groups = lax.axis_size("grp")
    cells = lax.axis_size("cell")
    ifaces, columns = load.shape[1:]
    prim = primal_basis.shape[1]
    owned, row_unknowns = group_inverse.shape[1:]
    coarsest_n = coarsest_inverse.shape[0]
    schur, local_inverse, basis = schur[0], local_inverse[0], primal_basis[0]
    face = ifaces // 4
    level = Level(prim, owned, row_unknowns, coarsest_n, columns)

    own = split_faces(load[0])
    got = exchange(own)
    orders = (face_map[0][:, :, None] == lax.iota(jnp.int32, face)[None, None, :]).astype(BF16)
    lift = basis.T
    index = primal_index.reshape(prim, 1)
    tail = level.tail(group_inverse[0], group_to_coarsest[0], primal_index)

    residual, half, sent = gather_primal(own, got, orders, basis, tail)
    gathered = lax.all_gather(sent, "cell", axis=0, tiled=False)
    sent, picked, up = lower_first(level, gathered, index, coarsest_inverse)
    ups = lax.all_gather(sent, "grp", axis=0, tiled=False)
    *own, picked = solve_first(half, local_inverse, lift, picked, up, ups)
    search, *own, sums = image_of(own, exchange(own), orders, schur, residual, ())
    image, _, sent = gather_primal(own, exchange(own), orders, basis, sums)
    again = lax.all_gather(sent, "cell", axis=0, tiled=False)
    sent = lower_second(level, gathered, index, ups, again)
    sent = lax.all_to_all(sent, "grp", 0, 0, tiled=True)
    *shared, residual, total = solve_second(residual, image, local_inverse, lift, picked, sent)
    second, *own, sums = image_of(shared, exchange(shared), orders, schur, residual, own)
    sums = jnp.broadcast_to(sums[None], (groups * cells, EXTRA, columns))
    got = exchange(own)
    sums = lax.all_to_all(sums, ("grp", "cell"), 0, 0, tiled=True)
    result, residual = finish(own, got, orders, search, second, residual, image, total, sums)
    return result[None], residual[None]


def solution(mesh):
    split_axes = ("grp", "cell")
    placed = (
        P(split_axes, None, None),
        P(split_axes, None, None),
        P(split_axes, None, None),
        P(split_axes, None, None),
        P(split_axes, None, None),
        P(split_axes, None),
        P("grp", "cell", None),
        P("grp", "cell", None),
        P(),
    )
    return jax.shard_map(
        body,
        mesh=mesh,
        in_specs=placed,
        out_specs=(P(split_axes, None, None), P(split_axes, None, None)),
        check_vma=False,
    )
```

```python
import functools

import jax
import jax.numpy as jnp
from jax import lax
from jax.experimental import pallas as pl
from jax.experimental.pallas import tpu as pltpu
from jax.sharding import PartitionSpec as P

HIGHEST = lax.Precision.HIGHEST
EXTRA = 8
FIRST = (0, 3)
F32, BF16 = jnp.float32, jnp.bfloat16
ANY = pl.BlockSpec(memory_space=pl.ANY)
VMEM = pl.BlockSpec(memory_space=pltpu.VMEM)


def high_dot(a, b):
    return jnp.dot(a, b, precision=HIGHEST)


def wide(a, b):
    return jnp.dot(a, b, preferred_element_type=F32)


def pairs(count, odd):
    return [p for i in range(odd, count - 1, 2) for p in ((i, i + 1), (i + 1, i))]


def exchange(parts):
    got = [None] * 4
    for slot in range(4):
        axis, odd = ("grp", "cell")[slot // 2], slot % 2
        got[slot] = lax.ppermute(parts[slot], axis, pairs(lax.axis_size(axis), odd))
    return got


def slots():
    faces, weights = [], []
    for axis, low in (("grp", 2), ("cell", 0)):
        index, count = lax.axis_index(axis), lax.axis_size(axis)
        odd = lax.rem(index, 2)
        for up in (1 - odd, odd):
            there = jnp.where(up == 1, index < count - 1, index > 0)
            faces.append(low + up)
            weights.append(jnp.where(there, 0.5, 1.0).astype(F32))
    return faces, weights


def rows_of(face, size):
    return pl.ds(pl.multiple_of(face * size, size), size)


def split(values):
    high = values.astype(BF16)
    low = (values - high.astype(F32)).astype(BF16)
    return jnp.concatenate([high, low], axis=1)


def exact(matrix, values):
    both = wide(matrix, split(values))
    half = both.shape[1] // 2
    return both[:, :half] + both[:, half:]


def column_sums(values):
    return jnp.sum(values, axis=0, keepdims=True)


def stacked(values, pieces):
    width = values.shape[1] // pieces
    return jnp.concatenate([values[:, k * width : (k + 1) * width] for k in range(pieces)], axis=0)


def beside(values, pieces):
    height = values.shape[0] // pieces
    return jnp.concatenate(
        [values[k * height : (k + 1) * height] for k in range(pieces)], axis=1
    )


def call(kernel, inputs, specs, outs, out_specs, scratch, flops, limit=12 * 2**20):
    moved = sum(a.size * a.dtype.itemsize for a in inputs)
    return pl.pallas_call(
        kernel,
        out_shape=outs,
        in_specs=specs,
        out_specs=out_specs,
        scratch_shapes=scratch,
        compiler_params=pltpu.CompilerParams(vmem_limit_bytes=limit),
        cost_estimate=pl.CostEstimate(flops=flops, bytes_accessed=moved // 8, transcendentals=0),
    )(*inputs)


def shape(*dims):
    return jax.ShapeDtypeStruct(dims, F32)


def split_faces(load):
    size, columns = load.shape[0] // 4, load.shape[1]

    def kernel(load_ref, *refs):
        outs, sems = refs[:4], refs[4]
        faces, _ = slots()
        copies = [
            pltpu.make_async_copy(load_ref.at[rows_of(faces[s], size)], outs[s], sems.at[s])
            for s in range(4)
        ]
        for copy in copies:
            copy.start()
        for copy in copies:
            copy.wait()

    return call(
        kernel,
        [load],
        [ANY],
        [shape(size, columns)] * 4,
        [VMEM] * 4,
        [pltpu.SemaphoreType.DMA((4,))],
        0,
    )


def assembled_first(own, got, orders):
    size, columns = own[0].shape
    count = len(FIRST)

    def kernel(*refs):
        faces, _ = slots()
        for k, s in enumerate(FIRST):
            refs[-1][k] = refs[k][...] + exact(refs[2 * count][faces[s]], refs[count + k][...])

    return call(
        kernel,
        [own[s] for s in FIRST] + [got[s] for s in FIRST] + [orders],
        [VMEM] * (2 * count + 1),
        shape(count, size, columns),
        VMEM,
        [],
        2 * 2 * count * size * columns * size,
    )


def assembled(s, first_ref, own_refs, got_refs, order_ref, face):
    if s in FIRST:
        return first_ref[FIRST.index(s)]
    return own_refs[s][...] + exact(order_ref[face], got_refs[s][...])


def gather_primal(own, got, orders, basis, tail):
    size, columns = own[0].shape
    prim = basis.shape[0]
    whole = (4 * size, columns)

    first = assembled_first(own, got, orders)
    last = [s for s in range(4) if s not in FIRST]
    own, got = [own[s] for s in last], [got[s] for s in last]
    count = len(last)

    def kernel(first_ref, *refs):
        spread = lambda part: {s: part[i] for i, s in enumerate(last)}
        own_refs, got_refs = spread(refs[:count]), spread(refs[count : 2 * count])
        refs = refs[2 * count :]
        order_ref, basis_ref, tail_ref, full_ref, half_ref, sent_ref = refs
        faces, weights = slots()
        sent_ref[prim:, :] = tail_ref[...]
        for s in range(4):
            full = assembled(s, first_ref, own_refs, got_refs, order_ref, faces[s])
            full_ref[s] = full
            half_ref[rows_of(faces[s], size), :] = (full * weights[s]).astype(BF16)
        sent_ref[:prim, :] = wide(basis_ref[...], half_ref[...])

    return call(
        kernel,
        [first, *own, *got, orders, basis, tail],
        [VMEM] * (4 + 2 * count),
        [
            shape(4, size, columns),
            jax.ShapeDtypeStruct(whole, BF16),
            shape(prim + tail.shape[0], columns),
        ],
        [VMEM] * 3,
        [],
        2 * 4 * size * columns * (2 * size + prim),
    )


class Level:
    def __init__(self, prim, owned, unknowns, coarsest, columns):
        self.prim, self.owned, self.unknowns, self.coarsest = prim, owned, unknowns, coarsest
        self.inverse_pieces, self.lift_pieces = unknowns // columns, columns // coarsest
        self.at_inverse = prim
        self.at_lift = self.at_inverse + owned * self.inverse_pieces
        self.at_index = self.at_lift + owned // self.lift_pieces
        self.columns = columns
        self.room = 10 * 2**20 + 32 * unknowns * unknowns

    def tail(self, inverse, lift, index):
        index = jnp.pad(index.astype(F32), ((0, 7), (0, self.columns - self.prim)))
        return jnp.concatenate(
            [stacked(inverse, self.inverse_pieces), beside(lift, self.lift_pieces), index], axis=0
        )

    def read(self, ref, cells):
        inverse, lift, index = [], [], []
        for cell in range(cells):
            inverse.append(beside(ref[cell, self.at_inverse : self.at_lift, :], self.inverse_pieces))
            lift.append(stacked(ref[cell, self.at_lift : self.at_index, :], self.lift_pieces))
            index.append(ref[cell, self.at_index : self.at_index + 1, : self.prim])
        inverse, lift = jnp.concatenate(inverse, axis=0), jnp.concatenate(lift, axis=0)
        index = jnp.concatenate(index, axis=1).astype(jnp.int32)
        rows = lax.broadcasted_iota(jnp.int32, (self.unknowns, cells * self.prim), 0)
        return inverse, lift, (rows == index).astype(F32)

    def primal(self, ref, cells):
        return jnp.concatenate([ref[cell, : self.prim, :] for cell in range(cells)], axis=0)

    def picks(self, ref):
        columns = lax.broadcasted_iota(jnp.int32, (self.prim, self.unknowns), 1)
        return (columns == ref[...]).astype(F32)


def lower_first(level, gathered, index, coarsest_inverse):
    cells, _, columns = gathered.shape

    def kernel(gathered_ref, index_ref, coarsest_ref, sent_ref, own_ref, up_ref):
        inverse, lift, spread = level.read(gathered_ref, cells)
        picks = level.picks(index_ref)
        coarse = high_dot(spread, level.primal(gathered_ref, cells))
        own_ref[...] = high_dot(high_dot(picks, inverse), coarse)
        up = high_dot(high_dot(picks, lift), coarsest_ref[...])
        up_ref[...] = up
        sent_ref[: level.coarsest, :] = high_dot(lift.T, coarse)
        sent_ref[level.coarsest :, :] = beside(up, level.lift_pieces)

    return call(
        kernel,
        [gathered, index, coarsest_inverse],
        [VMEM] * 3,
        [
            shape(level.coarsest + level.prim // level.lift_pieces, columns),
            shape(level.prim, columns),
            shape(level.prim, level.coarsest),
        ],
        [VMEM] * 3,
        [],
        0,
        level.room,
    )


def lower_second(level, gathered, index, ups, again):
    cells, block, columns = again.shape
    groups = ups.shape[0]

    def kernel(gathered_ref, index_ref, ups_ref, again_ref, sent_ref):
        inverse, lift, spread = level.read(gathered_ref, cells)
        picks = level.picks(index_ref)
        coarse = high_dot(spread, level.primal(again_ref, cells))
        own = high_dot(high_dot(picks, inverse), coarse)
        lowered = high_dot(lift.T, coarse)
        sums = again_ref[0, level.prim :, :]
        for cell in range(1, cells):
            sums = sums + again_ref[cell, level.prim :, :]
        mine = lax.axis_index("grp")
        for row in range(groups):
            up = stacked(ups_ref[row, level.coarsest :, :], level.lift_pieces)
            sent_ref[row, : level.prim, :] = high_dot(up, lowered) + jnp.where(
                mine == row, own, jnp.zeros_like(own)
            )
            sent_ref[row, level.prim :, :] = sums

    return call(
        kernel,
        [gathered, index, ups, again],
        [VMEM] * 4,
        shape(groups, block, columns),
        VMEM,
        [],
        0,
        level.room,
    )


def solve_first(half, matrix, lift, own, up, sent):
    n, columns = half.shape
    size = n // 4
    prim, coarsest_n = up.shape

    def kernel(half_ref, matrix_ref, lift_ref, own_ref, up_ref, sent_ref, *refs):
        outs, picked_ref = refs[:4], refs[4]
        faces, weights = slots()
        coarsest = jnp.sum(sent_ref[:, :coarsest_n, :], axis=0)
        picked = own_ref[...] + high_dot(up_ref[...], coarsest)
        picked_ref[...] = picked
        picked = split(picked)
        for s in range(4):
            rows = rows_of(faces[s], size)
            raised = wide(lift_ref[rows, :], picked)
            raised = raised[:, :columns] + raised[:, columns:]
            outs[s][...] = (wide(matrix_ref[rows, :], half_ref[...]) + raised) * weights[s]

    return call(
        kernel,
        [half, matrix, lift, own, up, sent],
        [VMEM] * 6,
        [shape(size, columns)] * 4 + [shape(prim, columns)],
        [VMEM] * 5,
        [],
        2 * n * columns * n,
    )


def solve_second(residual, image, matrix, lift, picked, sent):
    _, size, columns = residual.shape
    n = 4 * size
    prim = picked.shape[0]

    def kernel(residual_ref, image_ref, matrix_ref, lift_ref, picked_ref, sent_ref, *refs):
        outs, next_ref, total_ref, half_ref = refs[:4], refs[4], refs[5], refs[6]
        faces, weights = slots()
        total = jnp.sum(sent_ref[...], axis=0)
        total_ref[...] = total[prim:]
        alpha = total[prim : prim + 1] / total[prim + 1 : prim + 2]
        picked = split(picked_ref[...] - alpha * total[:prim])
        for s in range(4):
            res = residual_ref[s] - alpha * image_ref[s]
            next_ref[s] = res
            half_ref[rows_of(faces[s], size), :] = (res * weights[s]).astype(BF16)
        for s in range(4):
            rows = rows_of(faces[s], size)
            raised = wide(lift_ref[rows, :], picked)
            raised = raised[:, :columns] + raised[:, columns:]
            outs[s][...] = (wide(matrix_ref[rows, :], half_ref[...]) + raised) * weights[s]

    return call(
        kernel,
        [residual, image, matrix, lift, picked, sent],
        [VMEM] * 6,
        [shape(size, columns)] * 4
        + [shape(4, size, columns), shape(sent.shape[1] - prim, columns)],
        [VMEM] * 6,
        [pltpu.VMEM((n, columns), BF16)],
        2 * n * columns * n,
    )


def image_of(own, got, orders, matrix, residual, past, pieces):
    size, columns = own[0].shape
    n = 4 * size
    extra = len(past)

    first = assembled_first(own, got, orders)
    last = [s for s in range(4) if s not in FIRST]
    own, got = [own[s] for s in last], [got[s] for s in last]
    count = len(last)

    def kernel(first_ref, *refs):
        spread = lambda part: {s: part[i] for i, s in enumerate(last)}
        own_refs, got_refs = spread(refs[:count]), spread(refs[count : 2 * count])
        refs = refs[2 * count :]
        order_ref, matrix_ref, residual_ref = refs[:3]
        past_refs, refs = refs[3 : 3 + extra], refs[3 + extra :]
        search_ref, outs, sums_ref, half_ref = refs[0], refs[1:5], refs[5], refs[6]
        faces, weights = slots()
        for s in range(4):
            search = assembled(s, first_ref, own_refs, got_refs, order_ref, faces[s])
            search_ref[s] = search
            half_ref[rows_of(faces[s], size), :] = search.astype(BF16)
        sums = [jnp.zeros((1, columns), F32) for _ in range(4)]
        for s in range(4):
            image = wide(matrix_ref[rows_of(faces[s], size), :], half_ref[...])
            outs[s][...] = image
            search = search_ref[s]
            sums[0] += weights[s] * column_sums(residual_ref[s] * search)
            sums[1] += column_sums(search * image)
            if extra:
                sums[2] += column_sums(search * past_refs[s][...])
        sums = stacked(jnp.concatenate(sums, axis=0), pieces)
        rows = sums.shape[0]
        sums_ref[:rows, :] = sums
        if rows < EXTRA:
            sums_ref[rows:, :] = jnp.zeros((EXTRA - rows, columns // pieces), F32)

    return call(
        kernel,
        [first, *own, *got, orders, matrix, residual, *past],
        [VMEM] * (4 + 2 * count + extra),
        [shape(4, size, columns)]
        + [shape(size, columns)] * 4
        + [shape(EXTRA, columns // pieces)],
        [VMEM] * 6,
        [pltpu.VMEM((n, columns), BF16)],
        2 * n * columns * (n + 2 * size),
    )


def finish(own, got, orders, search, second, residual, image, total, sums):
    size, columns = own[0].shape
    n = 4 * size
    pieces = columns // sums.shape[2]

    def kernel(*refs):
        own_refs, got_refs, order_ref = refs[:4], refs[4:8], refs[8]
        search_ref, second_ref, residual_ref, image_ref, total_ref, sums_ref = refs[9:15]
        out_refs, (solution_buf, residual_buf, sems) = refs[15:17], refs[17:]
        faces, _ = slots()
        product, curvature = total_ref[0:1, :], total_ref[1:2, :]
        sums = beside(jnp.sum(sums_ref[...], axis=0)[: 4 * pieces], pieces)
        alpha = product / curvature
        beta = sums[0:1] / product
        alpha_next = sums[0:1] / (sums[1:2] + beta * (2.0 * sums[2:3] + beta * curvature))
        stores = []
        for s in range(4):
            rows = rows_of(faces[s], size)
            image = own_refs[s][...] + exact(order_ref[faces[s]], got_refs[s][...])
            residual_buf[s] = residual_ref[s] - alpha_next * (image + beta * image_ref[s])
            search = search_ref[s]
            solution_buf[s] = alpha * search + alpha_next * (second_ref[s] + beta * search)
            for k, buf in enumerate((solution_buf, residual_buf)):
                copy = pltpu.make_async_copy(buf.at[s], out_refs[k].at[rows], sems.at[2 * s + k])
                copy.start()
                stores.append(copy)
        for copy in stores:
            copy.wait()

    return call(
        kernel,
        [*own, *got, orders, search, second, residual, image, total, sums],
        [VMEM] * 15,
        [shape(n, columns)] * 2,
        [ANY] * 2,
        [
            pltpu.VMEM((4, size, columns), F32),
            pltpu.VMEM((4, size, columns), F32),
            pltpu.SemaphoreType.DMA((8,)),
        ],
        2 * n * columns * 2 * size,
    )


def body(
    load,
    schur,
    local_inverse,
    face_map,
    primal_basis,
    primal_index,
    group_inverse,
    group_to_coarsest,
    coarsest_inverse,
):
    groups = lax.axis_size("grp")
    cells = lax.axis_size("cell")
    ifaces, columns = load.shape[1:]
    prim = primal_basis.shape[1]
    owned, row_unknowns = group_inverse.shape[1:]
    coarsest_n = coarsest_inverse.shape[0]
    schur, local_inverse, basis = schur[0], local_inverse[0], primal_basis[0]
    face = ifaces // 4
    level = Level(prim, owned, row_unknowns, coarsest_n, columns)

    own = split_faces(load[0])
    got = exchange(own)
    orders = (face_map[0][:, :, None] == lax.iota(jnp.int32, face)[None, None, :]).astype(BF16)
    lift = basis.T
    index = primal_index.reshape(prim, 1)
    tail = level.tail(group_inverse[0], group_to_coarsest[0], primal_index)

    residual, half, sent = gather_primal(own, got, orders, basis, tail)
    gathered = lax.all_gather(sent, "cell", axis=0, tiled=False)
    sent, picked, up = lower_first(level, gathered, index, coarsest_inverse)
    ups = lax.all_gather(sent, "grp", axis=0, tiled=False)
    *own, picked = solve_first(half, local_inverse, lift, picked, up, ups)
    search, *own, sums = image_of(own, exchange(own), orders, schur, residual, (), 1)
    image, _, sent = gather_primal(own, exchange(own), orders, basis, sums)
    again = lax.all_gather(sent, "cell", axis=0, tiled=False)
    sent = lower_second(level, gathered, index, ups, again)
    sent = lax.all_to_all(sent, "grp", 0, 0, tiled=True)
    *shared, residual, total = solve_second(residual, image, local_inverse, lift, picked, sent)
    second, *own, sums = image_of(
        shared, exchange(shared), orders, schur, residual, own, max(columns // 128, 1)
    )
    got = exchange(own)
    sums = jnp.broadcast_to(sums[None], (groups * cells,) + sums.shape)
    sums = lax.all_to_all(sums, ("grp", "cell"), 0, 0, tiled=True)
    result, residual = finish(own, got, orders, search, second, residual, image, total, sums)
    return result[None], residual[None]


def solution(mesh):
    split_axes = ("grp", "cell")
    placed = (
        P(split_axes, None, None),
        P(split_axes, None, None),
        P(split_axes, None, None),
        P(split_axes, None, None),
        P(split_axes, None, None),
        P(split_axes, None),
        P("grp", "cell", None),
        P("grp", "cell", None),
        P(),
    )
    return jax.shard_map(
        body,
        mesh=mesh,
        in_specs=placed,
        out_specs=(P(split_axes, None, None), P(split_axes, None, None)),
        check_vma=False,
    )
```

```python
import functools

import jax
import jax.numpy as jnp
from jax import lax
from jax.experimental import pallas as pl
from jax.experimental.pallas import tpu as pltpu
from jax.sharding import PartitionSpec as P

HIGHEST = lax.Precision.HIGHEST
EXTRA = 8
FIRST = (3, 0)
ORDER = (3, 0, 1, 2)
F32, BF16 = jnp.float32, jnp.bfloat16
ANY = pl.BlockSpec(memory_space=pl.ANY)
VMEM = pl.BlockSpec(memory_space=pltpu.VMEM)


def high_dot(a, b):
    return jnp.dot(a, b, precision=HIGHEST)


def wide(a, b):
    return jnp.dot(a, b, preferred_element_type=F32)


def pairs(count, odd):
    return [p for i in range(odd, count - 1, 2) for p in ((i, i + 1), (i + 1, i))]


def exchange(parts):
    got = [None] * 4
    for slot in range(4):
        axis, odd = ("grp", "cell")[slot // 2], slot % 2
        got[slot] = lax.ppermute(parts[slot], axis, pairs(lax.axis_size(axis), odd))
    return got


def slots():
    faces, weights = [], []
    for axis, low in (("grp", 2), ("cell", 0)):
        index, count = lax.axis_index(axis), lax.axis_size(axis)
        odd = lax.rem(index, 2)
        for up in (1 - odd, odd):
            there = jnp.where(up == 1, index < count - 1, index > 0)
            faces.append(low + up)
            weights.append(jnp.where(there, 0.5, 1.0).astype(F32))
    return faces, weights


def rows_of(face, size):
    return pl.ds(pl.multiple_of(face * size, size), size)


def split(values):
    high = values.astype(BF16)
    low = (values - high.astype(F32)).astype(BF16)
    return jnp.concatenate([high, low], axis=1)


def exact(matrix, values):
    both = wide(matrix, split(values))
    half = both.shape[1] // 2
    return both[:, :half] + both[:, half:]


def column_sums(values):
    return jnp.sum(values, axis=0, keepdims=True)


def stacked(values, pieces):
    width = values.shape[1] // pieces
    return jnp.concatenate([values[:, k * width : (k + 1) * width] for k in range(pieces)], axis=0)


def beside(values, pieces):
    height = values.shape[0] // pieces
    return jnp.concatenate(
        [values[k * height : (k + 1) * height] for k in range(pieces)], axis=1
    )


def call(kernel, inputs, specs, outs, out_specs, scratch, flops, limit=12 * 2**20):
    moved = sum(a.size * a.dtype.itemsize for a in inputs)
    return pl.pallas_call(
        kernel,
        out_shape=outs,
        in_specs=specs,
        out_specs=out_specs,
        scratch_shapes=scratch,
        compiler_params=pltpu.CompilerParams(vmem_limit_bytes=limit),
        cost_estimate=pl.CostEstimate(flops=flops, bytes_accessed=moved // 8, transcendentals=0),
    )(*inputs)


def shape(*dims):
    return jax.ShapeDtypeStruct(dims, F32)


def split_faces(load):
    size, columns = load.shape[0] // 4, load.shape[1]

    def kernel(load_ref, *outs):
        faces, _ = slots()
        for s in range(4):
            outs[s][...] = load_ref[rows_of(faces[s], size), :]

    return call(kernel, [load], [VMEM], [shape(size, columns)] * 4, [VMEM] * 4, [], 0)


def assembled_first(own, got, orders):
    size, columns = own[0].shape
    count = len(FIRST)

    def kernel(*refs):
        faces, _ = slots()
        for k, s in enumerate(FIRST):
            refs[-1][k] = refs[k][...] + exact(refs[2 * count][faces[s]], refs[count + k][...])

    return call(
        kernel,
        [own[s] for s in FIRST] + [got[s] for s in FIRST] + [orders],
        [VMEM] * (2 * count + 1),
        shape(count, size, columns),
        VMEM,
        [],
        2 * 2 * count * size * columns * size,
    )


def assembled(s, first_ref, own_refs, got_refs, order_ref, face):
    if s in FIRST:
        return first_ref[FIRST.index(s)]
    return own_refs[s][...] + exact(order_ref[face], got_refs[s][...])


def gather_primal(own, got, orders, basis, tail, keep):
    size, columns = own[0].shape
    prim = basis.shape[0]
    whole = (4 * size, columns)

    first = assembled_first(own, got, orders)
    last = [s for s in range(4) if s not in FIRST]
    own, got = [own[s] for s in last], [got[s] for s in last]
    count = len(last)

    def kernel(first_ref, *refs):
        spread = lambda part: {s: part[i] for i, s in enumerate(last)}
        own_refs, got_refs = spread(refs[:count]), spread(refs[count : 2 * count])
        refs = refs[2 * count :]
        order_ref, basis_ref, tail_ref, full_ref, sent_ref, half_ref = refs
        faces, weights = slots()
        sent_ref[prim:, :] = tail_ref[...]
        for s in range(4):
            full = assembled(s, first_ref, own_refs, got_refs, order_ref, faces[s])
            full_ref[s] = full
            half_ref[rows_of(faces[s], size), :] = (full * weights[s]).astype(BF16)
        sent_ref[:prim, :] = wide(basis_ref[...], half_ref[...])

    return call(
        kernel,
        [first, *own, *got, orders, basis, tail],
        [VMEM] * (4 + 2 * count),
        [shape(4, size, columns), shape(prim + tail.shape[0], columns)]
        + [jax.ShapeDtypeStruct(whole, BF16)] * keep,
        [VMEM] * (2 + keep),
        [pltpu.VMEM(whole, BF16)] * (1 - keep),
        2 * 4 * size * columns * (2 * size + prim),
    )


class Level:
    def __init__(self, prim, owned, unknowns, coarsest, columns):
        self.prim, self.owned, self.unknowns, self.coarsest = prim, owned, unknowns, coarsest
        self.inverse_pieces, self.lift_pieces = unknowns // columns, columns // coarsest
        self.at_inverse = prim
        self.at_lift = self.at_inverse + owned * self.inverse_pieces
        self.at_index = self.at_lift + owned // self.lift_pieces
        self.columns = columns
        self.room = 10 * 2**20 + 32 * unknowns * unknowns

    def tail(self, inverse, lift, index):
        index = jnp.pad(index.astype(F32), ((0, 7), (0, self.columns - self.prim)))
        return jnp.concatenate(
            [stacked(inverse, self.inverse_pieces), beside(lift, self.lift_pieces), index], axis=0
        )

    def read(self, ref, cells):
        inverse, lift, index = [], [], []
        for cell in range(cells):
            inverse.append(beside(ref[cell, self.at_inverse : self.at_lift, :], self.inverse_pieces))
            lift.append(stacked(ref[cell, self.at_lift : self.at_index, :], self.lift_pieces))
            index.append(ref[cell, self.at_index : self.at_index + 1, : self.prim])
        inverse, lift = jnp.concatenate(inverse, axis=0), jnp.concatenate(lift, axis=0)
        index = jnp.concatenate(index, axis=1).astype(jnp.int32)
        rows = lax.broadcasted_iota(jnp.int32, (self.unknowns, cells * self.prim), 0)
        return inverse, lift, (rows == index).astype(F32)

    def primal(self, ref, cells):
        return jnp.concatenate([ref[cell, : self.prim, :] for cell in range(cells)], axis=0)

    def picks(self, ref):
        columns = lax.broadcasted_iota(jnp.int32, (self.prim, self.unknowns), 1)
        return (columns == ref[...]).astype(F32)


def lower_first(level, gathered, index, coarsest_inverse):
    cells, _, columns = gathered.shape

    def kernel(gathered_ref, index_ref, coarsest_ref, sent_ref, own_ref, up_ref):
        inverse, lift, spread = level.read(gathered_ref, cells)
        picks = level.picks(index_ref)
        coarse = high_dot(spread, level.primal(gathered_ref, cells))
        own_ref[...] = high_dot(high_dot(picks, inverse), coarse)
        up = high_dot(high_dot(picks, lift), coarsest_ref[...])
        up_ref[...] = up
        sent_ref[: level.coarsest, :] = high_dot(lift.T, coarse)
        sent_ref[level.coarsest :, :] = beside(up, level.lift_pieces)

    return call(
        kernel,
        [gathered, index, coarsest_inverse],
        [VMEM] * 3,
        [
            shape(level.coarsest + level.prim // level.lift_pieces, columns),
            shape(level.prim, columns),
            shape(level.prim, level.coarsest),
        ],
        [VMEM] * 3,
        [],
        0,
        level.room,
    )


def lower_second(level, gathered, index, ups, again):
    cells, block, columns = again.shape
    groups = ups.shape[0]

    def kernel(gathered_ref, index_ref, ups_ref, again_ref, sent_ref):
        inverse, lift, spread = level.read(gathered_ref, cells)
        picks = level.picks(index_ref)
        coarse = high_dot(spread, level.primal(again_ref, cells))
        own = high_dot(high_dot(picks, inverse), coarse)
        lowered = high_dot(lift.T, coarse)
        sums = again_ref[0, level.prim :, :]
        for cell in range(1, cells):
            sums = sums + again_ref[cell, level.prim :, :]
        mine = lax.axis_index("grp")
        for row in range(groups):
            up = stacked(ups_ref[row, level.coarsest :, :], level.lift_pieces)
            sent_ref[row, : level.prim, :] = high_dot(up, lowered) + jnp.where(
                mine == row, own, jnp.zeros_like(own)
            )
            sent_ref[row, level.prim :, :] = sums

    return call(
        kernel,
        [gathered, index, ups, again],
        [VMEM] * 4,
        shape(groups, block, columns),
        VMEM,
        [],
        0,
        level.room,
    )


def solve_first(half, matrix, lift, own, up, sent):
    n, columns = half.shape
    size = n // 4
    prim, coarsest_n = up.shape

    def kernel(half_ref, matrix_ref, lift_ref, own_ref, up_ref, sent_ref, *refs):
        outs, picked_ref = refs[:4], refs[4]
        faces, weights = slots()
        coarsest = jnp.sum(sent_ref[:, :coarsest_n, :], axis=0)
        picked = own_ref[...] + high_dot(up_ref[...], coarsest)
        picked_ref[...] = picked
        picked = split(picked)
        for s in range(4):
            rows = rows_of(faces[s], size)
            raised = wide(lift_ref[rows, :], picked)
            raised = raised[:, :columns] + raised[:, columns:]
            outs[s][...] = (wide(matrix_ref[rows, :], half_ref[...]) + raised) * weights[s]

    return call(
        kernel,
        [half, matrix, lift, own, up, sent],
        [VMEM] * 6,
        [shape(size, columns)] * 4 + [shape(prim, columns)],
        [VMEM] * 5,
        [],
        2 * n * columns * n,
    )


def solve_second(residual, image, matrix, lift, picked, sent):
    _, size, columns = residual.shape
    n = 4 * size
    prim = picked.shape[0]

    def kernel(residual_ref, image_ref, matrix_ref, lift_ref, picked_ref, sent_ref, *refs):
        outs, next_ref, total_ref, half_ref = refs[:4], refs[4], refs[5], refs[6]
        faces, weights = slots()
        total = jnp.sum(sent_ref[...], axis=0)
        total_ref[...] = total[prim:]
        alpha = total[prim : prim + 1] / total[prim + 1 : prim + 2]
        picked = split(picked_ref[...] - alpha * total[:prim])
        for s in range(4):
            res = residual_ref[s] - alpha * image_ref[s]
            next_ref[s] = res
            half_ref[rows_of(faces[s], size), :] = (res * weights[s]).astype(BF16)
        for s in range(4):
            rows = rows_of(faces[s], size)
            raised = wide(lift_ref[rows, :], picked)
            raised = raised[:, :columns] + raised[:, columns:]
            outs[s][...] = (wide(matrix_ref[rows, :], half_ref[...]) + raised) * weights[s]

    return call(
        kernel,
        [residual, image, matrix, lift, picked, sent],
        [VMEM] * 6,
        [shape(size, columns)] * 4
        + [shape(4, size, columns), shape(sent.shape[1] - prim, columns)],
        [VMEM] * 6,
        [pltpu.VMEM((n, columns), BF16)],
        2 * n * columns * n,
    )


def image_of(own, got, orders, matrix, residual, past, pieces):
    size, columns = own[0].shape
    n = 4 * size
    extra = len(past)

    first = assembled_first(own, got, orders)
    last = [s for s in range(4) if s not in FIRST]
    own, got = [own[s] for s in last], [got[s] for s in last]
    count = len(last)

    def kernel(first_ref, *refs):
        spread = lambda part: {s: part[i] for i, s in enumerate(last)}
        own_refs, got_refs = spread(refs[:count]), spread(refs[count : 2 * count])
        refs = refs[2 * count :]
        order_ref, matrix_ref, residual_ref = refs[:3]
        past_refs, refs = refs[3 : 3 + extra], refs[3 + extra :]
        search_ref, outs, sums_ref, half_ref = refs[0], refs[1:5], refs[5], refs[6]
        faces, weights = slots()
        for s in range(4):
            search = assembled(s, first_ref, own_refs, got_refs, order_ref, faces[s])
            search_ref[s] = search
            half_ref[rows_of(faces[s], size), :] = search.astype(BF16)
        sums = [jnp.zeros((1, columns), F32) for _ in range(4)]
        for s in range(4):
            image = wide(matrix_ref[rows_of(faces[s], size), :], half_ref[...])
            outs[s][...] = image
            search = search_ref[s]
            sums[0] += weights[s] * column_sums(residual_ref[s] * search)
            sums[1] += column_sums(search * image)
            if extra:
                sums[2] += column_sums(search * past_refs[s][...])
        sums = stacked(jnp.concatenate(sums, axis=0), pieces)
        rows = sums.shape[0]
        sums_ref[:rows, :] = sums
        if rows < EXTRA:
            sums_ref[rows:, :] = jnp.zeros((EXTRA - rows, columns // pieces), F32)

    return call(
        kernel,
        [first, *own, *got, orders, matrix, residual, *past],
        [VMEM] * (4 + 2 * count + extra),
        [shape(4, size, columns)]
        + [shape(size, columns)] * 4
        + [shape(EXTRA, columns // pieces)],
        [VMEM] * 6,
        [pltpu.VMEM((n, columns), BF16)],
        2 * n * columns * (n + 2 * size),
    )


def finish(own, got, orders, search, second, residual, image, total, sums):
    size, columns = own[0].shape
    n = 4 * size
    pieces = columns // sums.shape[2]

    def kernel(*refs):
        own_refs, order_ref = refs[:4], refs[8]
        got_refs = {s: refs[4 + k] for k, s in enumerate(ORDER)}
        search_ref, second_ref, residual_ref, image_ref, total_ref, sums_ref = refs[9:15]
        out_refs, (solution_buf, residual_buf, sems) = refs[15:17], refs[17:]
        faces, _ = slots()
        product, curvature = total_ref[0:1, :], total_ref[1:2, :]
        sums = beside(jnp.sum(sums_ref[...], axis=0)[: 4 * pieces], pieces)
        alpha = product / curvature
        beta = sums[0:1] / product
        alpha_next = sums[0:1] / (sums[1:2] + beta * (2.0 * sums[2:3] + beta * curvature))
        stores = []
        for s in range(4):
            rows = rows_of(faces[s], size)
            image = own_refs[s][...] + exact(order_ref[faces[s]], got_refs[s][...])
            residual_buf[s] = residual_ref[s] - alpha_next * (image + beta * image_ref[s])
            search = search_ref[s]
            solution_buf[s] = alpha * search + alpha_next * (second_ref[s] + beta * search)
            for k, buf in enumerate((solution_buf, residual_buf)):
                copy = pltpu.make_async_copy(buf.at[s], out_refs[k].at[rows], sems.at[2 * s + k])
                copy.start()
                stores.append(copy)
        for copy in stores:
            copy.wait()

    return call(
        kernel,
        [*own, *(got[s] for s in ORDER), orders, search, second, residual, image, total, sums],
        [VMEM] * 15,
        [shape(n, columns)] * 2,
        [ANY] * 2,
        [
            pltpu.VMEM((4, size, columns), F32),
            pltpu.VMEM((4, size, columns), F32),
            pltpu.SemaphoreType.DMA((8,)),
        ],
        2 * n * columns * 2 * size,
    )


def body(
    load,
    schur,
    local_inverse,
    face_map,
    primal_basis,
    primal_index,
    group_inverse,
    group_to_coarsest,
    coarsest_inverse,
):
    groups = lax.axis_size("grp")
    cells = lax.axis_size("cell")
    ifaces, columns = load.shape[1:]
    prim = primal_basis.shape[1]
    owned, row_unknowns = group_inverse.shape[1:]
    coarsest_n = coarsest_inverse.shape[0]
    schur, local_inverse, basis = schur[0], local_inverse[0], primal_basis[0]
    face = ifaces // 4
    level = Level(prim, owned, row_unknowns, coarsest_n, columns)

    own = split_faces(load[0])
    got = exchange(own)
    orders = (face_map[0][:, :, None] == lax.iota(jnp.int32, face)[None, None, :]).astype(BF16)
    lift = basis.T
    index = primal_index.reshape(prim, 1)
    tail = level.tail(group_inverse[0], group_to_coarsest[0], primal_index)

    residual, sent, half = gather_primal(own, got, orders, basis, tail, 1)
    gathered = lax.all_gather(sent, "cell", axis=0, tiled=False)
    sent, picked, up = lower_first(level, gathered, index, coarsest_inverse)
    ups = lax.all_gather(sent, "grp", axis=0, tiled=False)
    *own, picked = solve_first(half, local_inverse, lift, picked, up, ups)
    search, *own, sums = image_of(own, exchange(own), orders, schur, residual, (), 1)
    image, sent = gather_primal(own, exchange(own), orders, basis, sums, 0)
    again = lax.all_gather(sent, "cell", axis=0, tiled=False)
    sent = lower_second(level, gathered, index, ups, again)
    sent = lax.all_to_all(sent, "grp", 0, 0, tiled=True)
    *shared, residual, total = solve_second(residual, image, local_inverse, lift, picked, sent)
    second, *own, sums = image_of(
        shared, exchange(shared), orders, schur, residual, own, max(columns // 128, 1)
    )
    got = exchange(own)
    sums = jnp.broadcast_to(sums[None], (groups * cells,) + sums.shape)
    sums = lax.all_to_all(sums, ("grp", "cell"), 0, 0, tiled=True)
    result, residual = finish(own, got, orders, search, second, residual, image, total, sums)
    return result[None], residual[None]


def solution(mesh):
    split_axes = ("grp", "cell")
    placed = (
        P(split_axes, None, None),
        P(split_axes, None, None),
        P(split_axes, None, None),
        P(split_axes, None, None),
        P(split_axes, None, None),
        P(split_axes, None),
        P("grp", "cell", None),
        P("grp", "cell", None),
        P(),
    )
    return jax.shard_map(
        body,
        mesh=mesh,
        in_specs=placed,
        out_specs=(P(split_axes, None, None), P(split_axes, None, None)),
        check_vma=False,
    )
```
